32 devices in a mesh: groups: 2 (over x), seq: 8 (over z, y), head: 2 (over core).
Axes of the slice: x: 2, y: 2, z: 4, core: 2. Of those that a mesh axis runs over, the one named last changes fastest.
Arguments:
- byte_ids: int32 [8192], P(('groups', 'seq')), parts along dimension 0, may hold values from 0 to 255
- embed_table: bfloat16 [256, 1024], P(None, 'head'), may hold values from -6 to 6
- gains: float32 [2, 1024], replicated, may hold values from 0.1 to 1.9
- conv_weight: bfloat16 [2, 3, 1024, 1024], P(None, None, None, 'head'), may hold values from -0.109375 to 0.109375
- conv_bias: float32 [2, 1024], P(None, 'head'), may hold values from -3 to 3
- qkv_weight: bfloat16 [3, 1024, 2048], P(None, None, 'head'), may hold values from -5 to 5
Outputs:
- context: bfloat16 [1024, 2048], P(('groups', 'seq'), 'head'), parts along dimension 0
The draws below stay inside these ranges and needn't reach their ends.
There are 2 independent parts, one for each index of `groups`. The reference program is written for one: setup_inputs(seed, part) draws one part's arguments, and reference() takes and returns one part's arrays. A program takes and returns all parts, laid end to end along the dimension named above; an argument that names none is the same for every part. Nothing has to cross between parts.
All inputs are finite; a program needn't handle non-finite values.
Results may differ from the reference program's by a relative error of at most 0.0173.
The reference program's roundings to bfloat16 on the way (of `active` and `pooled`) count: a program that leaves them out, or rounds other values in their place, can miss the bound.
Values may be sent and summed in bfloat16 or wider, within the bound.
A program may use at most 128 MiB of HBM per device.

```python
import jax
import jax.numpy as jnp
from jax import lax

D = 1024
WIDTH = 2048
HEADS = 32
HEAD_SIZE = 64
VOCAB = 256
LAYERS = 2
DILATION_FIRST = 1024
DILATION_SECOND = 2048
POOL = 8
TOKENS = 4096
POOLED = 512


def draw_qkv_weight(key, part):
    entries = jnp.clip(jax.random.normal(jax.random.fold_in(key, 11), (3, D, WIDTH), jnp.float32), -4.0, 4.0) * D ** (-0.5)
    return entries.astype(jnp.bfloat16)


def touch_ends(drawn, own_key, smallest, largest):
    place = [jax.random.randint(jax.random.fold_in(own_key, axis), (), 0, length) for axis, length in enumerate(drawn.shape)]
    widest = drawn.shape.index(max(drawn.shape))
    neighbour = place[:widest] + [(place[widest] + 1) % drawn.shape[widest]] + place[widest + 1:]
    return drawn.at[tuple(place)].set(smallest).at[tuple(neighbour)].set(largest)


def block_scale(rng, shape, cuts, smallest, high):
    def one(position, shards_of):
        draws = jax.random.uniform(jax.random.fold_in(jax.random.fold_in(rng, 6), position), (shards_of,), jnp.float32, smallest / len(cuts), high / len(cuts))
        return jnp.repeat(jnp.exp(draws), shape[position] // shards_of).reshape((-1,) + (1,) * (len(shape) - position - 1))

    level = one(*cuts[0])
    for cut in cuts[1:]:
        level = level * one(*cut)
    return level


def bell_draw(stream_key, dims, spread, bound, pieces=(), kind=jnp.bfloat16):
    values = spread * jax.random.normal(stream_key, dims, jnp.float32)
    if pieces:
        values = values * block_scale(stream_key, dims, pieces, -0.22, 0.18)
    return jnp.clip(values, -bound, bound).astype(kind)


def setup_inputs(seed: int = 0, part: int = 0) -> dict:
    arg_keys = jax.random.split(jax.random.key(seed), 7)
    part_splits = jax.random.split(jax.random.fold_in(arg_keys[6], part), 7)
    byte_ids = touch_ends(jax.random.randint(part_splits[0], (TOKENS,), 0, VOCAB), jax.random.fold_in(part_splits[0], 1), 0, VOCAB - 1).astype(jnp.int32)
    embed_table = bell_draw(arg_keys[1], (VOCAB, D), 1.0, 6.0, ((1, 2),))
    gains = jnp.clip(1.0 + 0.18 * jax.random.normal(arg_keys[2], (LAYERS, D), jnp.float32), 0.1, 1.9)
    conv_weight = bell_draw(arg_keys[3], (LAYERS, 3, D, D), (3 * D) ** -0.5, 0.109375, ((3, 2),))
    conv_bias = bell_draw(arg_keys[4], (LAYERS, D), 0.5, 3.0, ((1, 2),), jnp.float32)
    qkv_weight = draw_qkv_weight(jax.random.fold_in(arg_keys[6], 71), part)
    return dict(byte_ids=byte_ids, embed_table=embed_table, gains=gains, conv_weight=conv_weight, conv_bias=conv_bias, qkv_weight=qkv_weight)


epsilon = 1e-05

def activate(stream, gain_row):
    rescale = lax.rsqrt(lax.optimization_barrier(jnp.mean(stream * stream, axis=1)) + epsilon)
    return jax.nn.gelu(stream * rescale[:, None] * gain_row[None, :], approximate=False).astype(jnp.bfloat16)

def one_head(operands):
    query_head, key_head, value_head = operands
    scores = jnp.dot(query_head, key_head.T, precision=lax.Precision.HIGHEST) * HEAD_SIZE ** (-0.5)
    places = jnp.arange(POOLED, dtype=jnp.int32)
    visible = places[None, :] <= places[:, None]
    masked = jnp.where(visible, scores, -jnp.inf)
    top_row = lax.optimization_barrier(jnp.max(masked, axis=1, keepdims=True))
    powers = jnp.where(visible, jnp.exp(masked - top_row), 0.0)
    totals = lax.optimization_barrier(jnp.sum(powers, axis=1, keepdims=True))
    return jnp.dot(powers, value_head, precision=lax.Precision.HIGHEST) / totals

def reference(byte_ids, embed_table, gains, conv_weight, conv_bias, qkv_weight):
    stream = embed_table[byte_ids].astype(jnp.float32)
    for layer_index, dilation_factor in enumerate((DILATION_FIRST, DILATION_SECOND)):
        active = activate(stream, gains[layer_index])
        padding = jnp.zeros((dilation_factor, D), jnp.bfloat16)
        behind = jnp.concatenate([padding, active[:-dilation_factor]], axis=0)
        in_front = jnp.concatenate([active[dilation_factor:], padding], axis=0)
        mixed = jnp.dot(behind, conv_weight[layer_index, 0], preferred_element_type=jnp.float32)
        mixed = mixed + jnp.dot(active, conv_weight[layer_index, 1], preferred_element_type=jnp.float32)
        mixed = mixed + jnp.dot(in_front, conv_weight[layer_index, 2], preferred_element_type=jnp.float32)
        stream = stream + mixed + conv_bias[layer_index][None, :]
    pooled = lax.optimization_barrier(jnp.mean(stream.reshape(POOLED, POOL, D), axis=1)).astype(jnp.bfloat16)

    def project(index):
        flat = jnp.dot(pooled, qkv_weight[index], preferred_element_type=jnp.float32).astype(jnp.bfloat16)
        return flat.reshape(POOLED, HEADS, HEAD_SIZE).transpose(1, 0, 2).astype(jnp.float32)
    queries = project(0)
    key_rows = project(1)
    value_rows = project(2)
    outputs = lax.map(one_head, (queries, key_rows, value_rows))
    return outputs.transpose(1, 0, 2).reshape(POOLED, WIDTH).astype(jnp.bfloat16)
```

```python
import functools

import jax
import jax.numpy as jnp
from jax import lax
from jax.experimental import pallas as pl
from jax.experimental.pallas import tpu as pltpu
from jax.sharding import PartitionSpec as P

HEAD_SIZE = 64
LAYERS = 2
DILATION_FIRST = 1024
POOL = 8
EPSILON = 1e-05
MESH = pl.DeviceIdType.MESH
F32 = jnp.float32
BF16 = jnp.bfloat16

ERF_P = (
    -2.72614225801306e-10,
    2.77068142495902e-08,
    -2.10102402082508e-06,
    -5.69250639462346e-05,
    -7.34990630326855e-04,
    -2.95459980854025e-03,
    -1.60960333262415e-02,
)
ERF_Q = (
    -1.45660718464996e-05,
    -2.13374055278905e-04,
    -1.68282697438203e-03,
    -7.37332916720468e-03,
    -1.42647390514189e-02,
)


def gelu(v):
    t = jnp.clip(v * 0.7071067811865476, -4.0, 4.0)
    t2 = t * t
    p = jnp.full_like(t2, ERF_P[0])
    for coefficient in ERF_P[1:]:
        p = p * t2 + coefficient
    q = jnp.full_like(t2, ERF_Q[0])
    for coefficient in ERF_Q[1:]:
        q = q * t2 + coefficient
    return 0.5 * v * (1.0 + t * p / q)


def inner_of(seq_count):
    inner = 1
    while (inner * 2) * (inner * 2) <= seq_count:
        inner *= 2
    return inner


def kernel(
    seq_count,
    ids_ref,
    table_ref,
    gains_ref,
    conv_hbm,
    bias_ref,
    qkv_hbm,
    out_ref,
    ids_buf,
    table_all,
    act_table,
    act,
    stream,
    acc,
    pooled_all,
    query_buf,
    key_buf,
    value_buf,
    conv_w,
    qkv_w,
    load_sem,
    ids_send,
    ids_recv,
    table_send,
    table_recv,
    stream_send,
    stream_recv,
    own_send,
    forward_send,
    core_send,
    block_recv,
    core_recv,
):
    pieces, _, cells = ids_ref.shape
    rows = pieces * cells
    vocab, half = table_ref.shape
    pooled_rows = rows // POOL
    inner = inner_of(seq_count)
    outer = seq_count // inner
    seq = lax.axis_index("seq")
    head = lax.axis_index("head")
    other = 1 - head
    outer_place = seq // inner
    inner_place = lax.rem(seq, inner)

    loads = [
        pltpu.make_async_copy(conv_hbm.at[0], conv_w.at[0], load_sem.at[0]),
        pltpu.make_async_copy(conv_hbm.at[1], conv_w.at[1], load_sem.at[1]),
        pltpu.make_async_copy(qkv_hbm, qkv_w, load_sem.at[2]),
    ]
    for load in loads:
        load.start()

    barrier = pltpu.get_barrier_semaphore()
    pl.semaphore_signal(barrier, inc=1, device_id={"head": other}, device_id_type=MESH)
    for step in range(1, seq_count):
        pl.semaphore_signal(
            barrier,
            inc=1,
            device_id={"seq": lax.rem(seq + step, seq_count)},
            device_id_type=MESH,
        )
    pl.semaphore_wait(barrier, seq_count)

    for piece in range(pieces):
        number = seq * pieces + piece
        target = lax.rem(number, seq_count)
        slot = number // seq_count

        @pl.when(target != seq)
        def _():
            pltpu.make_async_remote_copy(
                src_ref=ids_ref.at[piece],
                dst_ref=ids_buf.at[slot],
                send_sem=ids_send.at[piece],
                recv_sem=ids_recv.at[slot],
                device_id={"seq": target},
                device_id_type=MESH,
            ).start()

        @pl.when(target == seq)
        def _():
            pltpu.make_async_copy(
                ids_ref.at[piece], ids_buf.at[slot], ids_recv.at[slot]
            ).start()

    table_copy = pltpu.make_async_remote_copy(
        src_ref=table_ref,
        dst_ref=table_all.at[head],
        send_sem=table_send,
        recv_sem=table_recv,
        device_id={"head": other},
        device_id_type=MESH,
    )
    table_copy.start()
    table_all[head] = table_ref[...]
    table_copy.wait_recv()

    def activate(first, second, layer):
        total = jnp.sum(first * first, axis=1, keepdims=True) + jnp.sum(
            second * second, axis=1, keepdims=True
        )
        rescale = lax.rsqrt(total / (2 * half) + EPSILON)
        gain = gains_ref[layer : layer + 1, :]
        return (
            gelu(first * rescale * gain[:, :half]).astype(BF16),
            gelu(second * rescale * gain[:, half:]).astype(BF16),
        )

    CHUNK = 16
    UNROLL = 2

    @pl.loop(0, vocab // (CHUNK * UNROLL))
    def _(step):
        for part in range(UNROLL):
            place = pl.ds(pl.multiple_of((step * UNROLL + part) * CHUNK, CHUNK), CHUNK)
            first, second = activate(
                table_all[0, place, :].astype(F32), table_all[1, place, :].astype(F32), 0
            )
            act_table[place, :half] = first
            act_table[place, half:] = second

    vocab_ids = lax.broadcasted_iota(jnp.int32, (vocab, cells), 0)
    for piece in range(pieces):
        pltpu.make_async_copy(
            ids_ref.at[piece], ids_buf.at[piece], ids_recv.at[piece]
        ).wait()
        one_hot = (vocab_ids == ids_buf[piece]).astype(F32).astype(BF16)
        span = slice(piece * cells, (piece + 1) * cells)
        contract = (((0,), (0,)), ((), ()))
        stream[head, span, :] = lax.dot_general(
            one_hot, table_ref[...], contract, preferred_element_type=F32
        )
        act[span, :] = lax.dot_general(
            one_hot, act_table[...], contract, preferred_element_type=F32
        ).astype(BF16)

    def convolve(layer, step, start, stop):
        acc[start:stop, :] = (
            stream[head, start:stop, :]
            + bias_ref[layer : layer + 1, :]
            + jnp.dot(act[start:stop, :], conv_w[layer, 1], preferred_element_type=F32)
        )
        low = max(start, step)
        if low < stop:
            acc[low:stop, :] += jnp.dot(
                act[low - step : stop - step, :], conv_w[layer, 0], preferred_element_type=F32
            )
        high = min(stop, rows - step)
        if start < high:
            acc[start:high, :] += jnp.dot(
                act[start + step : high + step, :], conv_w[layer, 2], preferred_element_type=F32
            )

    PARTS = 2
    span_rows = rows // PARTS
    loads[0].wait()
    stream_copies = []
    for part in range(PARTS):
        start, stop = part * span_rows, (part + 1) * span_rows
        convolve(0, cells, start, stop)
        stream[head, start:stop, :] = acc[start:stop, :]
        copy = pltpu.make_async_remote_copy(
            src_ref=stream.at[head, pl.ds(start, span_rows)],
            dst_ref=stream.at[head, pl.ds(start, span_rows)],
            send_sem=stream_send.at[part],
            recv_sem=stream_recv.at[part],
            device_id={"head": other},
            device_id_type=MESH,
        )
        copy.start()
        stream_copies.append(copy)

    for part in range(PARTS):
        stream_copies[part].wait_recv()

        @pl.loop(0, span_rows // (CHUNK * UNROLL))
        def _(step):
            for chunk in range(UNROLL):
                place = pl.ds(
                    pl.multiple_of(part * span_rows + (step * UNROLL + chunk) * CHUNK, CHUNK),
                    CHUNK,
                )
                first, second = activate(stream[0, place, :], stream[1, place, :], 1)
                act[place, :half] = first
                act[place, half:] = second

    loads[1].wait()
    for part in range(PARTS):
        convolve(1, 2 * cells, part * span_rows, (part + 1) * span_rows)
    pooled_all[head, seq] = jnp.mean(
        acc[...].reshape(pooled_rows, POOL, half), axis=1
    ).astype(BF16)

    def push(block, device, send, recv):
        copy = pltpu.make_async_remote_copy(
            src_ref=pooled_all.at[head, block],
            dst_ref=pooled_all.at[head, block],
            send_sem=send,
            recv_sem=recv,
            device_id=device,
            device_id_type=MESH,
        )
        copy.start()
        return copy

    def arrived(block):
        pltpu.make_async_remote_copy(
            src_ref=pooled_all.at[head, block],
            dst_ref=pooled_all.at[head, block],
            send_sem=block_recv.at[block],
            recv_sem=block_recv.at[block],
            device_id={"head": other},
            device_id_type=MESH,
        ).wait_recv()

    sent = []
    for step in range(1, inner):
        target = outer_place * inner + lax.rem(inner_place + step, inner)
        sent.append(
            push(seq, {"seq": target}, forward_send.at[step - 1], block_recv.at[seq])
        )
    for step in range(1, outer):
        target = lax.rem(outer_place + step, outer) * inner + inner_place
        sent.append(push(seq, {"seq": target}, own_send.at[step - 1], block_recv.at[seq]))
    sent.append(push(seq, {"head": other}, core_send.at[0], core_recv.at[seq]))
    count = 1
    for step in range(1, outer):
        block = lax.rem(outer_place + outer - step, outer) * inner + inner_place
        arrived(block)
        for aside in range(1, inner):
            target = outer_place * inner + lax.rem(inner_place + aside, inner)
            sent.append(
                push(
                    block,
                    {"seq": target},
                    forward_send.at[step * (inner - 1) + aside - 1],
                    block_recv.at[block],
                )
            )
        sent.append(push(block, {"head": other}, core_send.at[count], core_recv.at[block]))
        count += 1
    for step in range(outer):
        for aside in range(1, inner):
            block = lax.rem(outer_place + outer - step, outer) * inner + lax.rem(
                inner_place + inner - aside, inner
            )
            arrived(block)
            sent.append(push(block, {"head": other}, core_send.at[count], core_recv.at[block]))
            count += 1
    for block in range(seq_count):
        pltpu.make_async_remote_copy(
            src_ref=pooled_all.at[other, block],
            dst_ref=pooled_all.at[other, block],
            send_sem=core_recv.at[block],
            recv_sem=core_recv.at[block],
            device_id={"head": other},
            device_id_type=MESH,
        ).wait_recv()

    loads[2].wait()
    whole = seq_count * pooled_rows
    width = qkv_w.shape[2]
    stride = cells // POOL
    period = DILATION_FIRST // POOL

    def position(place):
        source = place // pooled_rows
        within = lax.rem(place, pooled_rows)
        return within // stride * period + source * stride + lax.rem(within, stride)

    key_pos = position(lax.broadcasted_iota(jnp.int32, (pooled_rows, whole), 1))
    query_pos = seq * pooled_rows + lax.broadcasted_iota(jnp.int32, (pooled_rows, whole), 0)
    pick = (key_pos == query_pos).astype(F32).astype(BF16)
    sides = [pooled_all[side].reshape(whole, half) for side in range(2)]
    picked = [
        jnp.dot(pick, side, preferred_element_type=F32).astype(BF16) for side in sides
    ]
    TILE = 256
    for column in range(0, width, TILE):
        columns = slice(column, column + TILE)
        query_buf[:, columns] = (
            jnp.dot(picked[0], qkv_w[0, :half, columns], preferred_element_type=F32)
            + jnp.dot(picked[1], qkv_w[0, half:, columns], preferred_element_type=F32)
        ).astype(BF16)

    BAND = 8 * pooled_rows if seq_count % 8 == 0 else pooled_rows

    @pl.loop(0, whole // BAND)
    def _(band):
        blocks = pl.ds(band * (BAND // pooled_rows), BAND // pooled_rows)
        left = pooled_all[0, blocks].reshape(BAND, half)
        right = pooled_all[1, blocks].reshape(BAND, half)
        place = pl.ds(pl.multiple_of(band * BAND, BAND), BAND)
        for kind, target in ((1, key_buf), (2, value_buf)):
            for column in range(0, width, TILE):
                columns = slice(column, column + TILE)
                target[place, columns] = (
                    jnp.dot(left, qkv_w[kind, :half, columns], preferred_element_type=F32)
                    + jnp.dot(right, qkv_w[kind, half:, columns], preferred_element_type=F32)
                ).astype(BF16)

    PAIR = 2 * HEAD_SIZE
    lane = lax.broadcasted_iota(jnp.int32, (pooled_rows, PAIR), 1)
    left_lanes = lane < HEAD_SIZE
    visible = key_pos <= query_pos
    visible = jnp.concatenate([visible.astype(F32)] * 2, axis=0) > 0.5
    zero = jnp.zeros((pooled_rows, PAIR), F32)
    for column in range(0, width, PAIR):
        columns = slice(column, column + PAIR)
        query = query_buf[:, columns].astype(F32) * HEAD_SIZE ** (-0.5)
        stacked = jnp.concatenate(
            [jnp.where(left_lanes, query, zero), jnp.where(left_lanes, zero, query)], axis=0
        ).astype(BF16)
        scores = lax.dot_general(
            stacked, key_buf[:, columns], (((1,), (1,)), ((), ())), preferred_element_type=F32
        )
        scores = jnp.where(visible, scores, -1e30)
        top = jnp.max(scores, axis=1, keepdims=True)
        powers = jnp.where(visible, jnp.exp(scores - top), 0.0)
        total = jnp.sum(powers, axis=1, keepdims=True)
        weighted = (
            jnp.dot(powers.astype(BF16), value_buf[:, columns], preferred_element_type=F32)
            / total
        )
        out_ref[:, columns] = jnp.where(
            left_lanes, weighted[:pooled_rows], weighted[pooled_rows:]
        ).astype(BF16)

    for piece in range(pieces):
        target = lax.rem(seq * pieces + piece, seq_count)

        @pl.when(target != seq)
        def _():
            pltpu.make_async_remote_copy(
                src_ref=ids_ref.at[piece],
                dst_ref=ids_buf.at[0],
                send_sem=ids_send.at[piece],
                recv_sem=ids_recv.at[0],
                device_id={"seq": target},
                device_id_type=MESH,
            ).wait_send()

    table_copy.wait_send()
    for copy in stream_copies:
        copy.wait_send()
    for copy in sent:
        copy.wait_send()


def local(byte_ids, embed_table, gains, conv_weight, conv_bias, qkv_weight):
    seq_count = lax.axis_size("seq")
    rows = byte_ids.shape[0]
    vocab, half = embed_table.shape
    depth = conv_weight.shape[2]
    cells = DILATION_FIRST // seq_count
    pieces = rows // cells
    pooled_rows = rows // POOL
    width = qkv_weight.shape[2]
    whole = seq_count * pooled_rows
    inner = inner_of(seq_count)
    outer = seq_count // inner
    dma = pltpu.SemaphoreType.DMA
    vmem = pl.BlockSpec(memory_space=pltpu.VMEM)
    hbm = pl.BlockSpec(memory_space=pl.ANY)
    return pl.pallas_call(
        functools.partial(kernel, seq_count),
        out_shape=jax.ShapeDtypeStruct((pooled_rows, width), BF16),
        in_specs=[vmem, vmem, vmem, hbm, vmem, hbm],
        out_specs=vmem,
        scratch_shapes=[
            pltpu.VMEM((pieces, 1, cells), jnp.int32),
            pltpu.VMEM((2, vocab, half), BF16),
            pltpu.VMEM((vocab, depth), BF16),
            pltpu.VMEM((rows, depth), BF16),
            pltpu.VMEM((2, rows, half), F32),
            pltpu.VMEM((rows, half), F32),
            pltpu.VMEM((2, seq_count, pooled_rows, half), BF16),
            pltpu.VMEM((pooled_rows, width), BF16),
            pltpu.VMEM((whole, width), BF16),
            pltpu.VMEM((whole, width), BF16),
            pltpu.VMEM(conv_weight.shape, BF16),
            pltpu.VMEM(qkv_weight.shape, BF16),
            dma((3,)),
            dma((pieces,)),
            dma((pieces,)),
            dma,
            dma,
            dma((2,)),
            dma((2,)),
            dma((max(outer - 1, 1),)),
            dma((max(outer * (inner - 1), 1),)),
            dma((seq_count,)),
            dma((seq_count,)),
            dma((seq_count,)),
        ],
        compiler_params=pltpu.CompilerParams(
            collective_id=0, has_side_effects=True, vmem_limit_bytes=58 * 1024 * 1024
        ),
        name="stem",
    )(
        byte_ids.reshape(pieces, 1, cells),
        embed_table,
        gains,
        conv_weight,
        conv_bias,
        qkv_weight,
    )


def solution(mesh):
    placed = (
        P(("groups", "seq")),
        P(None, "head"),
        P(),
        P(None, None, None, "head"),
        P(None, "head"),
        P(None, None, "head"),
    )
    return jax.shard_map(
        local, mesh=mesh, in_specs=placed, out_specs=P(("groups", "seq"), "head"), check_vma=False
    )
```

```python
import functools

import jax
import jax.numpy as jnp
from jax import lax
from jax.experimental import pallas as pl
from jax.experimental.pallas import tpu as pltpu
from jax.sharding import PartitionSpec as P

HEAD_SIZE = 64
LAYERS = 2
DILATION_FIRST = 1024
POOL = 8
EPSILON = 1e-05
MESH = pl.DeviceIdType.MESH
F32 = jnp.float32
BF16 = jnp.bfloat16

ERF_P = (
    -2.72614225801306e-10,
    2.77068142495902e-08,
    -2.10102402082508e-06,
    -5.69250639462346e-05,
    -7.34990630326855e-04,
    -2.95459980854025e-03,
    -1.60960333262415e-02,
)
ERF_Q = (
    -1.45660718464996e-05,
    -2.13374055278905e-04,
    -1.68282697438203e-03,
    -7.37332916720468e-03,
    -1.42647390514189e-02,
)


def gelu(v):
    t = jnp.clip(v * 0.7071067811865476, -4.0, 4.0)
    t2 = t * t
    p = jnp.full_like(t2, ERF_P[0])
    for coefficient in ERF_P[1:]:
        p = p * t2 + coefficient
    q = jnp.full_like(t2, ERF_Q[0])
    for coefficient in ERF_Q[1:]:
        q = q * t2 + coefficient
    return 0.5 * v * (1.0 + t * p / q)


def inner_of(seq_count):
    inner = 1
    while (inner * 2) * (inner * 2) <= seq_count:
        inner *= 2
    return inner


def kernel(
    seq_count,
    ids_ref,
    table_ref,
    gains_ref,
    conv_hbm,
    bias_ref,
    qkv_hbm,
    out_ref,
    ids_buf,
    table_all,
    act_table,
    act,
    stream,
    acc,
    pooled_all,
    query_buf,
    key_buf,
    value_buf,
    conv_w,
    qkv_w,
    load_sem,
    ids_send,
    ids_recv,
    table_send,
    table_recv,
    stream_send,
    stream_recv,
    up_send,
    down_send,
    aside_send,
    core_send,
    block_recv,
    core_recv,
):
    pieces, _, cells = ids_ref.shape
    rows = pieces * cells
    vocab, half = table_ref.shape
    pooled_rows = rows // POOL
    inner = inner_of(seq_count)
    outer = seq_count // inner
    seq = lax.axis_index("seq")
    head = lax.axis_index("head")
    other = 1 - head
    outer_place = seq // inner
    inner_place = lax.rem(seq, inner)

    barrier = pltpu.get_barrier_semaphore()
    pl.semaphore_signal(barrier, inc=1, device_id={"head": other}, device_id_type=MESH)
    for step in range(1, seq_count):
        pl.semaphore_signal(
            barrier,
            inc=1,
            device_id={"seq": lax.rem(seq + step, seq_count)},
            device_id_type=MESH,
        )
    loads = [
        pltpu.make_async_copy(conv_hbm.at[0], conv_w.at[0], load_sem.at[0]),
        pltpu.make_async_copy(conv_hbm.at[1], conv_w.at[1], load_sem.at[1]),
        pltpu.make_async_copy(qkv_hbm, qkv_w, load_sem.at[2]),
    ]
    for load in loads:
        load.start()

    pl.semaphore_wait(barrier, seq_count)

    for piece in range(pieces):
        number = seq * pieces + piece
        target = lax.rem(number, seq_count)
        slot = number // seq_count

        @pl.when(target != seq)
        def _():
            pltpu.make_async_remote_copy(
                src_ref=ids_ref.at[piece],
                dst_ref=ids_buf.at[slot],
                send_sem=ids_send.at[piece],
                recv_sem=ids_recv.at[slot],
                device_id={"seq": target},
                device_id_type=MESH,
            ).start()

        @pl.when(target == seq)
        def _():
            pltpu.make_async_copy(
                ids_ref.at[piece], ids_buf.at[slot], ids_recv.at[slot]
            ).start()

    table_copy = pltpu.make_async_remote_copy(
        src_ref=table_ref,
        dst_ref=table_all.at[head],
        send_sem=table_send,
        recv_sem=table_recv,
        device_id={"head": other},
        device_id_type=MESH,
    )
    table_copy.start()
    table_all[head] = table_ref[...]
    table_copy.wait_recv()

    def activate(first, second, layer):
        total = jnp.sum(first * first, axis=1, keepdims=True) + jnp.sum(
            second * second, axis=1, keepdims=True
        )
        rescale = lax.rsqrt(total / (2 * half) + EPSILON)
        gain = gains_ref[layer : layer + 1, :]
        return (
            gelu(first * rescale * gain[:, :half]).astype(BF16),
            gelu(second * rescale * gain[:, half:]).astype(BF16),
        )

    CHUNK = 16
    UNROLL = 2

    @pl.loop(0, vocab // (CHUNK * UNROLL))
    def _(step):
        for part in range(UNROLL):
            place = pl.ds(pl.multiple_of((step * UNROLL + part) * CHUNK, CHUNK), CHUNK)
            first, second = activate(
                table_all[0, place, :].astype(F32), table_all[1, place, :].astype(F32), 0
            )
            act_table[place, :half] = first
            act_table[place, half:] = second

    vocab_ids = lax.broadcasted_iota(jnp.int32, (vocab, cells), 0)
    for piece in range(pieces):
        pltpu.make_async_copy(
            ids_ref.at[piece], ids_buf.at[piece], ids_recv.at[piece]
        ).wait()
        one_hot = (vocab_ids == ids_buf[piece]).astype(F32).astype(BF16)
        span = slice(piece * cells, (piece + 1) * cells)
        contract = (((0,), (0,)), ((), ()))
        stream[head, span, :] = lax.dot_general(
            one_hot, table_ref[...], contract, preferred_element_type=F32
        )
        act[span, :] = lax.dot_general(
            one_hot, act_table[...], contract, preferred_element_type=F32
        ).astype(BF16)

    def convolve(layer, step, start, stop):
        acc[start:stop, :] = (
            stream[head, start:stop, :]
            + bias_ref[layer : layer + 1, :]
            + jnp.dot(act[start:stop, :], conv_w[layer, 1], preferred_element_type=F32)
        )
        low = max(start, step)
        if low < stop:
            acc[low:stop, :] += jnp.dot(
                act[low - step : stop - step, :], conv_w[layer, 0], preferred_element_type=F32
            )
        high = min(stop, rows - step)
        if start < high:
            acc[start:high, :] += jnp.dot(
                act[start + step : high + step, :], conv_w[layer, 2], preferred_element_type=F32
            )

    PARTS = 2
    span_rows = rows // PARTS
    loads[0].wait()
    stream_copies = []
    for part in range(PARTS):
        start, stop = part * span_rows, (part + 1) * span_rows
        convolve(0, cells, start, stop)
        stream[head, start:stop, :] = acc[start:stop, :]
        copy = pltpu.make_async_remote_copy(
            src_ref=stream.at[head, pl.ds(start, span_rows)],
            dst_ref=stream.at[head, pl.ds(start, span_rows)],
            send_sem=stream_send.at[part],
            recv_sem=stream_recv.at[part],
            device_id={"head": other},
            device_id_type=MESH,
        )
        copy.start()
        stream_copies.append(copy)

    for part in range(PARTS):
        stream_copies[part].wait_recv()

        @pl.loop(0, span_rows // (CHUNK * UNROLL))
        def _(step):
            for chunk in range(UNROLL):
                place = pl.ds(
                    pl.multiple_of(part * span_rows + (step * UNROLL + chunk) * CHUNK, CHUNK),
                    CHUNK,
                )
                first, second = activate(stream[0, place, :], stream[1, place, :], 1)
                act[place, :half] = first
                act[place, half:] = second

    loads[1].wait()
    for part in range(PARTS):
        convolve(1, 2 * cells, part * span_rows, (part + 1) * span_rows)
    own = inner_place * outer + outer_place
    pooled_all[head, own] = jnp.mean(
        acc[...].reshape(pooled_rows, POOL, half), axis=1
    ).astype(BF16)

    def in_order(step, act_on):
        if step == 0:
            act_on(outer_place)
            return

        @pl.when(outer_place - step >= 0)
        def _():
            act_on(outer_place - step)

        @pl.when(outer_place + step < outer)
        def _():
            act_on(outer_place + step)

    def push(block, device, send, recv):
        return pltpu.make_async_remote_copy(
            src_ref=pooled_all.at[head, block],
            dst_ref=pooled_all.at[head, block],
            send_sem=send,
            recv_sem=recv,
            device_id=device,
            device_id_type=MESH,
        )

    def up(block):
        target = lax.rem(outer_place + 1, outer) * inner + inner_place
        return push(block, {"seq": target}, up_send.at[block], block_recv.at[block])

    def down(block):
        target = lax.rem(outer_place + outer - 1, outer) * inner + inner_place
        return push(block, {"seq": target}, down_send.at[block], block_recv.at[block])

    def aside(step, block):
        target = outer_place * inner + lax.rem(inner_place + step, inner)
        return push(block, {"seq": target}, aside_send.at[step - 1, block], block_recv.at[block])

    def across(block):
        return push(block, {"head": other}, core_send.at[block], core_recv.at[block])

    def arrived(block):
        push(block, {"head": other}, core_send.at[block], block_recv.at[block]).wait_recv()

    def column_block(place):
        block = inner_place * outer + place

        @pl.when(place != outer_place)
        def _():
            arrived(block)

        @pl.when(jnp.logical_and(place <= outer_place, outer_place < outer - 1))
        def _():
            up(block).start()

        @pl.when(jnp.logical_and(place >= outer_place, outer_place > 0))
        def _():
            down(block).start()

        for step in range(1, inner):
            aside(step, block).start()
        across(block).start()

    def aside_block(place):
        for step in range(1, inner):
            block = lax.rem(inner_place + inner - step, inner) * outer + place
            arrived(block)
            across(block).start()

    def crossed(column):
        for place in range(outer):
            block = column * outer + place
            pltpu.make_async_remote_copy(
                src_ref=pooled_all.at[other, block],
                dst_ref=pooled_all.at[other, block],
                send_sem=core_send.at[block],
                recv_sem=core_recv.at[block],
                device_id={"head": other},
                device_id_type=MESH,
            ).wait_recv()

    for step in range(outer):
        in_order(step, column_block)
    loads[2].wait()
    whole = seq_count * pooled_rows
    width = qkv_w.shape[2]
    stride = cells // POOL
    period = DILATION_FIRST // POOL
    TILE = 256
    BAND = outer * pooled_rows

    def keys_values(column, between):
        blocks = pl.ds(column * outer, outer)
        place = pl.ds(pl.multiple_of(column * BAND, BAND), BAND)
        done = 0
        for kind, target in ((1, key_buf), (2, value_buf)):
            for start in range(0, width, TILE):
                columns = slice(start, start + TILE)
                target[place, columns] = (
                    jnp.dot(
                        pooled_all[0, blocks].reshape(BAND, half),
                        qkv_w[kind, :half, columns],
                        preferred_element_type=F32,
                    )
                    + jnp.dot(
                        pooled_all[1, blocks].reshape(BAND, half),
                        qkv_w[kind, half:, columns],
                        preferred_element_type=F32,
                    )
                ).astype(BF16)
                between(done)
                done += 1

    tiles = 2 * (width // TILE)

    def between(done):
        for step in range(outer):
            if done == min(2 * step, tiles - 1):
                in_order(step, aside_block)

    crossed(inner_place)
    keys_values(inner_place, between)

    @pl.loop(1, inner)
    def _(step):
        column = lax.rem(inner_place + step, inner)
        crossed(column)
        keys_values(column, lambda done: None)

    def position(place):
        block = place // pooled_rows
        source = lax.rem(block, outer) * inner + block // outer
        within = lax.rem(place, pooled_rows)
        return within // stride * period + source * stride + lax.rem(within, stride)

    key_pos = position(lax.broadcasted_iota(jnp.int32, (pooled_rows, whole), 1))
    query_pos = seq * pooled_rows + lax.broadcasted_iota(jnp.int32, (pooled_rows, whole), 0)
    pick = (key_pos == query_pos).astype(F32).astype(BF16)
    sides = [pooled_all[side].reshape(whole, half) for side in range(2)]
    picked = [
        jnp.dot(pick, side, preferred_element_type=F32).astype(BF16) for side in sides
    ]
    for column in range(0, width, TILE):
        columns = slice(column, column + TILE)
        query_buf[:, columns] = (
            jnp.dot(picked[0], qkv_w[0, :half, columns], preferred_element_type=F32)
            + jnp.dot(picked[1], qkv_w[0, half:, columns], preferred_element_type=F32)
        ).astype(BF16)

    PAIR = 2 * HEAD_SIZE
    lane = lax.broadcasted_iota(jnp.int32, (pooled_rows, PAIR), 1)
    left_lanes = lane < HEAD_SIZE
    visible = key_pos <= query_pos
    visible = jnp.concatenate([visible.astype(F32)] * 2, axis=0) > 0.5
    zero = jnp.zeros((pooled_rows, PAIR), F32)
    for column in range(0, width, PAIR):
        columns = slice(column, column + PAIR)
        query = query_buf[:, columns].astype(F32) * HEAD_SIZE ** (-0.5)
        stacked = jnp.concatenate(
            [jnp.where(left_lanes, query, zero), jnp.where(left_lanes, zero, query)], axis=0
        ).astype(BF16)
        scores = lax.dot_general(
            stacked, key_buf[:, columns], (((1,), (1,)), ((), ())), preferred_element_type=F32
        )
        scores = jnp.where(visible, scores, -1e30)
        top = jnp.max(scores, axis=1, keepdims=True)
        powers = jnp.where(visible, jnp.exp(scores - top), 0.0)
        total = jnp.sum(powers, axis=1, keepdims=True)
        weighted = (
            jnp.dot(powers.astype(BF16), value_buf[:, columns], preferred_element_type=F32)
            / total
        )
        out_ref[:, columns] = jnp.where(
            left_lanes, weighted[:pooled_rows], weighted[pooled_rows:]
        ).astype(BF16)

    for piece in range(pieces):
        target = lax.rem(seq * pieces + piece, seq_count)

        @pl.when(target != seq)
        def _():
            pltpu.make_async_remote_copy(
                src_ref=ids_ref.at[piece],
                dst_ref=ids_buf.at[0],
                send_sem=ids_send.at[piece],
                recv_sem=ids_recv.at[0],
                device_id={"seq": target},
                device_id_type=MESH,
            ).wait_send()

    table_copy.wait_send()
    for copy in stream_copies:
        copy.wait_send()
    for place in range(outer):
        block = inner_place * outer + place

        @pl.when(jnp.logical_and(place <= outer_place, outer_place < outer - 1))
        def _():
            up(block).wait_send()

        @pl.when(jnp.logical_and(place >= outer_place, outer_place > 0))
        def _():
            down(block).wait_send()

        for step in range(1, inner):
            aside(step, block).wait_send()
    for block in range(seq_count):
        across(block).wait_send()


def local(byte_ids, embed_table, gains, conv_weight, conv_bias, qkv_weight):
    seq_count = lax.axis_size("seq")
    rows = byte_ids.shape[0]
    vocab, half = embed_table.shape
    depth = conv_weight.shape[2]
    cells = DILATION_FIRST // seq_count
    pieces = rows // cells
    pooled_rows = rows // POOL
    width = qkv_weight.shape[2]
    whole = seq_count * pooled_rows
    inner = inner_of(seq_count)
    outer = seq_count // inner
    dma = pltpu.SemaphoreType.DMA
    vmem = pl.BlockSpec(memory_space=pltpu.VMEM)
    hbm = pl.BlockSpec(memory_space=pl.ANY)
    return pl.pallas_call(
        functools.partial(kernel, seq_count),
        out_shape=jax.ShapeDtypeStruct((pooled_rows, width), BF16),
        in_specs=[vmem, vmem, vmem, hbm, vmem, hbm],
        out_specs=vmem,
        scratch_shapes=[
            pltpu.VMEM((pieces, 1, cells), jnp.int32),
            pltpu.VMEM((2, vocab, half), BF16),
            pltpu.VMEM((vocab, depth), BF16),
            pltpu.VMEM((rows, depth), BF16),
            pltpu.VMEM((2, rows, half), F32),
            pltpu.VMEM((rows, half), F32),
            pltpu.VMEM((2, seq_count, pooled_rows, half), BF16),
            pltpu.VMEM((pooled_rows, width), BF16),
            pltpu.VMEM((whole, width), BF16),
            pltpu.VMEM((whole, width), BF16),
            pltpu.VMEM(conv_weight.shape, BF16),
            pltpu.VMEM(qkv_weight.shape, BF16),
            dma((3,)),
            dma((pieces,)),
            dma((pieces,)),
            dma,
            dma,
            dma((2,)),
            dma((2,)),
            dma((seq_count,)),
            dma((seq_count,)),
            dma((max(inner - 1, 1), seq_count)),
            dma((seq_count,)),
            dma((seq_count,)),
            dma((seq_count,)),
        ],
        compiler_params=pltpu.CompilerParams(
            collective_id=0, has_side_effects=True, vmem_limit_bytes=58 * 1024 * 1024
        ),
        name="stem",
    )(
        byte_ids.reshape(pieces, 1, cells),
        embed_table,
        gains,
        conv_weight,
        conv_bias,
        qkv_weight,
    )


def solution(mesh):
    placed = (
        P(("groups", "seq")),
        P(None, "head"),
        P(),
        P(None, None, None, "head"),
        P(None, "head"),
        P(None, None, "head"),
    )
    return jax.shard_map(
        local, mesh=mesh, in_specs=placed, out_specs=P(("groups", "seq"), "head"), check_vma=False
    )
```

```python
import functools

import jax
import jax.numpy as jnp
from jax import lax
from jax.experimental import pallas as pl
from jax.experimental.pallas import tpu as pltpu
from jax.sharding import PartitionSpec as P

HEAD_SIZE = 64
LAYERS = 2
DILATION_FIRST = 1024
POOL = 8
EPSILON = 1e-05
MESH = pl.DeviceIdType.MESH
F32 = jnp.float32
BF16 = jnp.bfloat16

ERF_P = (
    -2.72614225801306e-10,
    2.77068142495902e-08,
    -2.10102402082508e-06,
    -5.69250639462346e-05,
    -7.34990630326855e-04,
    -2.95459980854025e-03,
    -1.60960333262415e-02,
)
ERF_Q = (
    -1.45660718464996e-05,
    -2.13374055278905e-04,
    -1.68282697438203e-03,
    -7.37332916720468e-03,
    -1.42647390514189e-02,
)


def gelu(v):
    t = jnp.clip(v * 0.7071067811865476, -4.0, 4.0)
    t2 = t * t
    p = jnp.full_like(t2, ERF_P[0])
    for coefficient in ERF_P[1:]:
        p = p * t2 + coefficient
    q = jnp.full_like(t2, ERF_Q[0])
    for coefficient in ERF_Q[1:]:
        q = q * t2 + coefficient
    return 0.5 * v * (1.0 + t * p / q)


def inner_of(seq_count):
    inner = 1
    while (inner * 2) * (inner * 2) <= seq_count:
        inner *= 2
    return inner


def kernel(
    seq_count,
    ids_ref,
    table_ref,
    gains_ref,
    conv_hbm,
    bias_ref,
    qkv_hbm,
    out_ref,
    ids_buf,
    table_all,
    act_table,
    act,
    stream,
    acc,
    pooled_all,
    query_buf,
    key_buf,
    value_buf,
    conv_w,
    qkv_w,
    load_sem,
    ids_send,
    ids_recv,
    table_send,
    table_recv,
    stream_send,
    stream_recv,
    along_send,
    aside_send,
    core_send,
    block_recv,
    core_recv,
):
    pieces, _, cells = ids_ref.shape
    rows = pieces * cells
    vocab, half = table_ref.shape
    pooled_rows = rows // POOL
    inner = inner_of(seq_count)
    outer = seq_count // inner
    seq = lax.axis_index("seq")
    head = lax.axis_index("head")
    other = 1 - head
    outer_place = seq // inner
    inner_place = lax.rem(seq, inner)

    barrier = pltpu.get_barrier_semaphore()
    pl.semaphore_signal(barrier, inc=1, device_id={"head": other}, device_id_type=MESH)
    for step in range(1, seq_count):
        pl.semaphore_signal(
            barrier,
            inc=1,
            device_id={"seq": lax.rem(seq + step, seq_count)},
            device_id_type=MESH,
        )
    loads = [
        pltpu.make_async_copy(conv_hbm.at[0], conv_w.at[0], load_sem.at[0]),
        pltpu.make_async_copy(conv_hbm.at[1], conv_w.at[1], load_sem.at[1]),
        pltpu.make_async_copy(qkv_hbm, qkv_w, load_sem.at[2]),
    ]
    for load in loads:
        load.start()

    pl.semaphore_wait(barrier, seq_count)

    for piece in range(pieces):
        number = seq * pieces + piece
        target = lax.rem(number, seq_count)
        slot = number // seq_count

        @pl.when(target != seq)
        def _():
            pltpu.make_async_remote_copy(
                src_ref=ids_ref.at[piece],
                dst_ref=ids_buf.at[slot],
                send_sem=ids_send.at[piece],
                recv_sem=ids_recv.at[slot],
                device_id={"seq": target},
                device_id_type=MESH,
            ).start()

        @pl.when(target == seq)
        def _():
            pltpu.make_async_copy(
                ids_ref.at[piece], ids_buf.at[slot], ids_recv.at[slot]
            ).start()

    table_copy = pltpu.make_async_remote_copy(
        src_ref=table_ref,
        dst_ref=table_all.at[head],
        send_sem=table_send,
        recv_sem=table_recv,
        device_id={"head": other},
        device_id_type=MESH,
    )
    table_copy.start()
    table_all[head] = table_ref[...]
    table_copy.wait_recv()

    def activate(first, second, layer):
        total = jnp.sum(first * first, axis=1, keepdims=True) + jnp.sum(
            second * second, axis=1, keepdims=True
        )
        rescale = lax.rsqrt(total / (2 * half) + EPSILON)
        gain = gains_ref[layer : layer + 1, :]
        return (
            gelu(first * rescale * gain[:, :half]).astype(BF16),
            gelu(second * rescale * gain[:, half:]).astype(BF16),
        )

    CHUNK = 16
    UNROLL = 4

    @pl.loop(0, vocab // (CHUNK * UNROLL))
    def _(step):
        for part in range(UNROLL):
            place = pl.ds(pl.multiple_of((step * UNROLL + part) * CHUNK, CHUNK), CHUNK)
            first, second = activate(
                table_all[0, place, :].astype(F32), table_all[1, place, :].astype(F32), 0
            )
            act_table[place, :half] = first
            act_table[place, half:] = second

    vocab_ids = lax.broadcasted_iota(jnp.int32, (vocab, cells), 0)
    for piece in range(pieces):
        pltpu.make_async_copy(
            ids_ref.at[piece], ids_buf.at[piece], ids_recv.at[piece]
        ).wait()
        one_hot = (vocab_ids == ids_buf[piece]).astype(F32).astype(BF16)
        span = slice(piece * cells, (piece + 1) * cells)
        contract = (((0,), (0,)), ((), ()))
        stream[head, span, :] = lax.dot_general(
            one_hot, table_ref[...], contract, preferred_element_type=F32
        )
        act[span, :] = lax.dot_general(
            one_hot, act_table[...], contract, preferred_element_type=F32
        ).astype(BF16)

    def convolve(layer, step, start, stop):
        acc[start:stop, :] = (
            stream[head, start:stop, :]
            + bias_ref[layer : layer + 1, :]
            + jnp.dot(act[start:stop, :], conv_w[layer, 1], preferred_element_type=F32)
        )
        low = max(start, step)
        if low < stop:
            acc[low:stop, :] += jnp.dot(
                act[low - step : stop - step, :], conv_w[layer, 0], preferred_element_type=F32
            )
        high = min(stop, rows - step)
        if start < high:
            acc[start:high, :] += jnp.dot(
                act[start + step : high + step, :], conv_w[layer, 2], preferred_element_type=F32
            )

    PARTS = 2
    span_rows = rows // PARTS
    loads[0].wait()
    stream_copies = []
    for part in range(PARTS):
        start, stop = part * span_rows, (part + 1) * span_rows
        convolve(0, cells, start, stop)
        stream[head, start:stop, :] = acc[start:stop, :]
        copy = pltpu.make_async_remote_copy(
            src_ref=stream.at[head, pl.ds(start, span_rows)],
            dst_ref=stream.at[head, pl.ds(start, span_rows)],
            send_sem=stream_send.at[part],
            recv_sem=stream_recv.at[part],
            device_id={"head": other},
            device_id_type=MESH,
        )
        copy.start()
        stream_copies.append(copy)

    for part in range(PARTS):
        stream_copies[part].wait_recv()

        @pl.loop(0, span_rows // (CHUNK * UNROLL))
        def _(step):
            for chunk in range(UNROLL):
                place = pl.ds(
                    pl.multiple_of(part * span_rows + (step * UNROLL + chunk) * CHUNK, CHUNK),
                    CHUNK,
                )
                first, second = activate(stream[0, place, :], stream[1, place, :], 1)
                act[place, :half] = first
                act[place, half:] = second

    loads[1].wait()
    for part in range(PARTS):
        convolve(1, 2 * cells, part * span_rows, (part + 1) * span_rows)
    own = inner_place * outer + outer_place
    pooled_all[head, own] = jnp.mean(
        acc[...].reshape(pooled_rows, POOL, half), axis=1
    ).astype(BF16)

    def in_order(step, act_on):
        if step == 0:
            act_on(outer_place)
            return

        @pl.when(outer_place - step >= 0)
        def _():
            act_on(outer_place - step)

        @pl.when(outer_place + step < outer)
        def _():
            act_on(outer_place + step)

    def push(block, device, send, recv):
        return pltpu.make_async_remote_copy(
            src_ref=pooled_all.at[head, block],
            dst_ref=pooled_all.at[head, block],
            send_sem=send,
            recv_sem=recv,
            device_id=device,
            device_id_type=MESH,
        )

    def along(step):
        target = lax.rem(outer_place + step, outer) * inner + inner_place
        return push(own, {"seq": target}, along_send.at[step - 1], block_recv.at[own])

    def aside(step, block):
        target = outer_place * inner + lax.rem(inner_place + step, inner)
        return push(block, {"seq": target}, aside_send.at[step - 1, block], block_recv.at[block])

    def across(block):
        return push(block, {"head": other}, core_send.at[block], core_recv.at[block])

    def arrived(block):
        push(block, {"head": other}, core_send.at[block], block_recv.at[block]).wait_recv()

    def column_block(place):
        block = inner_place * outer + place

        @pl.when(place != outer_place)
        def _():
            arrived(block)

        for step in range(1, inner):
            aside(step, block).start()
        across(block).start()

    def aside_block(place):
        for step in range(1, inner):
            block = lax.rem(inner_place + inner - step, inner) * outer + place
            arrived(block)
            across(block).start()

    def crossed(column):
        for place in range(outer):
            block = column * outer + place
            pltpu.make_async_remote_copy(
                src_ref=pooled_all.at[other, block],
                dst_ref=pooled_all.at[other, block],
                send_sem=core_send.at[block],
                recv_sem=core_recv.at[block],
                device_id={"head": other},
                device_id_type=MESH,
            ).wait_recv()

    for step in range(1, outer):
        along(step).start()
    for step in range(outer):
        in_order(step, column_block)
    loads[2].wait()
    whole = seq_count * pooled_rows
    width = qkv_w.shape[2]
    stride = cells // POOL
    period = DILATION_FIRST // POOL
    TILE = 256
    BAND = outer * pooled_rows

    def keys_values(column, between):
        blocks = pl.ds(column * outer, outer)
        place = pl.ds(pl.multiple_of(column * BAND, BAND), BAND)
        done = 0
        for kind, target in ((1, key_buf), (2, value_buf)):
            for start in range(0, width, TILE):
                columns = slice(start, start + TILE)
                target[place, columns] = (
                    jnp.dot(
                        pooled_all[0, blocks].reshape(BAND, half),
                        qkv_w[kind, :half, columns],
                        preferred_element_type=F32,
                    )
                    + jnp.dot(
                        pooled_all[1, blocks].reshape(BAND, half),
                        qkv_w[kind, half:, columns],
                        preferred_element_type=F32,
                    )
                ).astype(BF16)
                between(done)
                done += 1

    tiles = 2 * (width // TILE)

    def between(done):
        for step in range(outer):
            if done == min(2 * step, tiles - 1):
                in_order(step, aside_block)

    crossed(inner_place)
    keys_values(inner_place, between)

    @pl.loop(1, inner)
    def _(step):
        column = lax.rem(inner_place + step, inner)
        crossed(column)
        keys_values(column, lambda done: None)

    def position(place):
        block = place // pooled_rows
        source = lax.rem(block, outer) * inner + block // outer
        within = lax.rem(place, pooled_rows)
        return within // stride * period + source * stride + lax.rem(within, stride)

    key_pos = position(lax.broadcasted_iota(jnp.int32, (pooled_rows, whole), 1))
    query_pos = seq * pooled_rows + lax.broadcasted_iota(jnp.int32, (pooled_rows, whole), 0)
    pick = (key_pos == query_pos).astype(F32).astype(BF16)
    sides = [pooled_all[side].reshape(whole, half) for side in range(2)]
    picked = [
        jnp.dot(pick, side, preferred_element_type=F32).astype(BF16) for side in sides
    ]
    for column in range(0, width, TILE):
        columns = slice(column, column + TILE)
        query_buf[:, columns] = (
            jnp.dot(picked[0], qkv_w[0, :half, columns], preferred_element_type=F32)
            + jnp.dot(picked[1], qkv_w[0, half:, columns], preferred_element_type=F32)
        ).astype(BF16)

    PAIR = 2 * HEAD_SIZE
    lane = lax.broadcasted_iota(jnp.int32, (pooled_rows, PAIR), 1)
    left_lanes = lane < HEAD_SIZE
    visible = key_pos <= query_pos
    visible = jnp.concatenate([visible.astype(F32)] * 2, axis=0) > 0.5
    zero = jnp.zeros((pooled_rows, PAIR), F32)
    for column in range(0, width, PAIR):
        columns = slice(column, column + PAIR)
        query = query_buf[:, columns].astype(F32) * HEAD_SIZE ** (-0.5)
        stacked = jnp.concatenate(
            [jnp.where(left_lanes, query, zero), jnp.where(left_lanes, zero, query)], axis=0
        ).astype(BF16)
        scores = lax.dot_general(
            stacked, key_buf[:, columns], (((1,), (1,)), ((), ())), preferred_element_type=F32
        )
        scores = jnp.where(visible, scores, -1e30)
        top = jnp.max(scores, axis=1, keepdims=True)
        powers = jnp.where(visible, jnp.exp(scores - top), 0.0)
        total = jnp.sum(powers, axis=1, keepdims=True)
        weighted = (
            jnp.dot(powers.astype(BF16), value_buf[:, columns], preferred_element_type=F32)
            / total
        )
        out_ref[:, columns] = jnp.where(
            left_lanes, weighted[:pooled_rows], weighted[pooled_rows:]
        ).astype(BF16)

    for piece in range(pieces):
        target = lax.rem(seq * pieces + piece, seq_count)

        @pl.when(target != seq)
        def _():
            pltpu.make_async_remote_copy(
                src_ref=ids_ref.at[piece],
                dst_ref=ids_buf.at[0],
                send_sem=ids_send.at[piece],
                recv_sem=ids_recv.at[0],
                device_id={"seq": target},
                device_id_type=MESH,
            ).wait_send()

    table_copy.wait_send()
    for copy in stream_copies:
        copy.wait_send()
    for place in range(outer):
        block = inner_place * outer + place

        for step in range(1, inner):
            aside(step, block).wait_send()
    for step in range(1, outer):
        along(step).wait_send()
    for block in range(seq_count):
        across(block).wait_send()


def local(byte_ids, embed_table, gains, conv_weight, conv_bias, qkv_weight):
    seq_count = lax.axis_size("seq")
    rows = byte_ids.shape[0]
    vocab, half = embed_table.shape
    depth = conv_weight.shape[2]
    cells = DILATION_FIRST // seq_count
    pieces = rows // cells
    pooled_rows = rows // POOL
    width = qkv_weight.shape[2]
    whole = seq_count * pooled_rows
    inner = inner_of(seq_count)
    outer = seq_count // inner
    dma = pltpu.SemaphoreType.DMA
    vmem = pl.BlockSpec(memory_space=pltpu.VMEM)
    hbm = pl.BlockSpec(memory_space=pl.ANY)
    return pl.pallas_call(
        functools.partial(kernel, seq_count),
        out_shape=jax.ShapeDtypeStruct((pooled_rows, width), BF16),
        in_specs=[vmem, vmem, vmem, hbm, vmem, hbm],
        out_specs=vmem,
        scratch_shapes=[
            pltpu.VMEM((pieces, 1, cells), jnp.int32),
            pltpu.VMEM((2, vocab, half), BF16),
            pltpu.VMEM((vocab, depth), BF16),
            pltpu.VMEM((rows, depth), BF16),
            pltpu.VMEM((2, rows, half), F32),
            pltpu.VMEM((rows, half), F32),
            pltpu.VMEM((2, seq_count, pooled_rows, half), BF16),
            pltpu.VMEM((pooled_rows, width), BF16),
            pltpu.VMEM((whole, width), BF16),
            pltpu.VMEM((whole, width), BF16),
            pltpu.VMEM(conv_weight.shape, BF16),
            pltpu.VMEM(qkv_weight.shape, BF16),
            dma((3,)),
            dma((pieces,)),
            dma((pieces,)),
            dma,
            dma,
            dma((2,)),
            dma((2,)),
            dma((max(outer - 1, 1),)),
            dma((max(inner - 1, 1), seq_count)),
            dma((seq_count,)),
            dma((seq_count,)),
            dma((seq_count,)),
        ],
        compiler_params=pltpu.CompilerParams(
            collective_id=0, has_side_effects=True, vmem_limit_bytes=58 * 1024 * 1024
        ),
        name="stem",
    )(
        byte_ids.reshape(pieces, 1, cells),
        embed_table,
        gains,
        conv_weight,
        conv_bias,
        qkv_weight,
    )


def solution(mesh):
    placed = (
        P(("groups", "seq")),
        P(None, "head"),
        P(),
        P(None, None, None, "head"),
        P(None, "head"),
        P(None, None, "head"),
    )
    return jax.shard_map(
        local, mesh=mesh, in_specs=placed, out_specs=P(("groups", "seq"), "head"), check_vma=False
    )
```
